256 devices in a mesh: head: 8 (over z), outer: 4 (over y_lo, core), inner: 8 (over y_hi, x).
Axes of the slice: x: 4, y: 4 (y_hi: 2, y_lo: 2; y = y_hi * 2 + y_lo), z: 8, core: 2. Of those that a mesh axis runs over, the one named last changes fastest.
Arguments:
- queries: bfloat16 [4, 3072, 4096], P('outer', ('inner', 'head')), may hold values from -90 to 90
- keys: bfloat16 [4, 3072, 4096], P('outer', ('inner', 'head')), may hold values from -3 to 3
- values: bfloat16 [4, 3072, 4096], P('outer', ('inner', 'head')), may hold values from -6 to 6
- out_grad: bfloat16 [4, 3072, 4096], P('outer', ('inner', 'head')), may hold values from -6 to 6
- outputs: bfloat16 [4, 3072, 4096], P('outer', ('inner', 'head')), may hold values from -3 to 3
- doc_ids: int32 [4, 24], P('outer'), may hold values from 0 to 7, never falling along the last dimension, each value on 1 to 12 neighbouring positions
- block_order: int32 [4, 24], P('outer'), may hold values from 0 to 23, each once within a row
Outputs:
- query_grad: bfloat16 [4, 3072, 4096], P('outer', ('inner', 'head'))
- key_grad: bfloat16 [4, 3072, 4096], P('outer', ('inner', 'head'))
- value_grad: bfloat16 [4, 3072, 4096], P('outer', ('inner', 'head'))
The draws below stay inside these ranges and needn't reach their ends.
Inputs may be any that keep to these rules, and one draw needn't show every extreme that they name: `doc_ids`: never falling along a window's sequence; in each window one document spans 12 blocks. `block_order`: each sequence block of a window appears once in its row.
All inputs are finite; a program needn't handle non-finite values.
Results may differ from the reference program's by a relative error of at most 0.0049.
Values may be sent and summed in bfloat16 or wider, within the bound.
No kernel may reach another device: no remote copies, remote signals or barrier semaphores. Data moves between devices by JAX's collectives and lax.ppermute only.
A program may use at most 64 MiB of HBM per device.

```python
import math
import jax
import jax.numpy as jnp
import numpy as np
from jax import lax

HEADS = 32
HD = 128
BLOCK = 128
BATCH = 4
TOKENS = 3072
NBLK = 24


def shared_keys(key):
    base_keys = jnp.clip(jax.random.normal(key, (BATCH, TOKENS, HEADS * HD), jnp.float32), -3.0, 3.0)
    return base_keys


def draw_keys(key, part):
    base_keys = shared_keys(key)
    key = jax.random.fold_in(key, 7)
    row_scale = jnp.exp(jax.random.uniform(key, (BATCH, TOKENS, 1), jnp.float32, -0.7, 0.7))
    return jnp.clip(base_keys * row_scale, -3.0, 3.0).astype(jnp.bfloat16)


def draw_queries(key, part):
    key = jax.random.fold_in(key, 5)
    normal_draw = jax.random.normal(key, (BATCH, TOKENS, HEADS * HD), jnp.float32)
    return jnp.clip(1.5 * normal_draw, -3.0, 3.0).astype(jnp.bfloat16)


def steps_of(own_key, shape, pieces, smallest, high):
    level, own = 1.0, jax.random.fold_in(own_key, 6)
    for dim, parts in pieces:
        steps = jnp.exp(jax.random.uniform(jax.random.fold_in(own, dim), (parts,), jnp.float32, smallest / len(pieces), high / len(pieces)))
        level = level * jnp.repeat(steps, shape[dim] // parts).reshape([-1 if axis == dim else 1 for axis in range(len(shape))])
    return level


def profile(number_of, total, most, slope):
    weights = [(1 << 20) // math.isqrt(standing ** slope) + 1 for standing in range(2, number_of + 1)]
    surplus, given = total - most - (number_of - 1), [1] * (number_of - 1)
    while surplus > 0:
        movable = [i for i in range(number_of - 1) if given[i] < most]
        pool, budget = sum([weights[i] for i in movable]), surplus
        for i in movable:
            extra = min(most - given[i], max(1, budget * weights[i] // pool), surplus)
            given[i] = given[i] + extra
            surplus = surplus - extra
    return np.array([most] + given)


def uneven_parts(key, count, total, limit, skew):
    if count == 2:
        one = jax.random.randint(key, (), max(1, total - limit), min(limit, total - 1) + 1)
        return jnp.stack([one, total - one])
    tallies = jnp.asarray(profile(count, total, limit, skew), jnp.int32)
    pairs = (count - 1) // 2
    giver, taker = tallies[1:1 + 2 * pairs:2], tallies[2:2 + 2 * pairs:2]
    room = jnp.minimum(giver - 1, limit - taker)
    passed = jax.random.randint(jax.random.fold_in(key, 1), (pairs,), 0, 1 << 20) % (room + 1)
    tallies = tallies.at[1:1 + 2 * pairs:2].set(giver - passed).at[2:2 + 2 * pairs:2].set(taker + passed)
    return tallies[jax.random.permutation(jax.random.fold_in(key, 2), count)]


def normal_values(own_key, extent, scale, reach, cuts=(), kind=jnp.bfloat16):
    entries = scale * jax.random.normal(own_key, extent, jnp.float32)
    if cuts:
        entries = entries * steps_of(own_key, extent, cuts, -0.22, 0.18)
    return jnp.clip(entries, -reach, reach).astype(kind)


def setup_inputs(seed: int = 0) -> dict:
    key_list = jax.random.split(jax.random.key(seed), 8)
    return {
        "queries": draw_queries(jax.random.fold_in(key_list[7], 71), 0),
        "keys": draw_keys(jax.random.fold_in(key_list[7], 71), 0),
        "values": normal_values(key_list[2], (BATCH, TOKENS, HEADS * HD), 1.0, 6.0, ((0, 4), (1, 64))),
        "out_grad": normal_values(key_list[3], (BATCH, TOKENS, HEADS * HD), 1.0, 6.0, ((0, 4), (1, 64))),
        "outputs": normal_values(key_list[4], (BATCH, TOKENS, HEADS * HD), 0.5, 3.0, ((0, 4), (1, 64))),
        "doc_ids": jax.vmap(lambda own: jnp.searchsorted(jnp.cumsum(uneven_parts(own, max(NBLK // 3, 2), NBLK, NBLK // 2, 2)), jnp.arange(NBLK), side="right"))(jax.random.split(key_list[5], BATCH)).reshape((BATCH, NBLK)).astype(jnp.int32),
        "block_order": jax.vmap(lambda own: jax.random.permutation(own, NBLK))(jax.random.split(key_list[6], BATCH)).reshape((BATCH, NBLK)).astype(jnp.int32),
    }


NEG_FILL = -1e+30

def window_backward(inputs):
    queries, keys, values, out_grad, outputs, doc_ids, block_order = inputs
    score_scale = 1.0 / math.sqrt(HD)
    block_count = TOKENS // BLOCK
    sequence = jnp.arange(TOKENS, dtype=jnp.int32)
    holder = jnp.zeros((block_count,), jnp.int32).at[block_order].set(jnp.arange(block_count, dtype=jnp.int32))
    stored = holder[sequence // BLOCK] * BLOCK + sequence % BLOCK
    documents = doc_ids[sequence // BLOCK]
    positions = block_order[sequence // BLOCK] * BLOCK + sequence % BLOCK

    def heads_first(matrix):
        return matrix[stored].reshape(TOKENS, HEADS, HD).transpose(1, 0, 2)

    def one_head(head_inputs):
        query_seq, key_seq, value_seq, grad_seq, output_seq = head_inputs
        out_dot = lax.optimization_barrier(jnp.sum(grad_seq.astype(jnp.float32) * output_seq.astype(jnp.float32), axis=1))
        key_grad = jnp.zeros((TOKENS, HD), jnp.float32)
        value_grad = jnp.zeros((TOKENS, HD), jnp.float32)
        query_pieces = []
        block_span = min(1024, TOKENS)
        for block_start in range(0, TOKENS, block_span):
            block_end = min(block_start + block_span, TOKENS)
            allowed = (sequence[None, :block_end] <= sequence[block_start:block_end, None]) & (documents[None, :block_end] == documents[block_start:block_end, None])
            scores = jnp.dot(query_seq[block_start:block_end], key_seq[:block_end].T, preferred_element_type=jnp.float32) * score_scale
            scores = jnp.where(allowed, scores, NEG_FILL)
            highest = lax.optimization_barrier(jnp.max(scores, axis=1, keepdims=True))
            log_total = highest + jnp.log(lax.optimization_barrier(jnp.sum(jnp.exp(scores - highest), axis=1, keepdims=True)))
            weights = jnp.where(allowed, jnp.exp(scores - log_total), 0.0)
            weights_low = weights.astype(jnp.bfloat16)
            grad_block = grad_seq[block_start:block_end]
            value_grad = value_grad.at[:block_end].add(jnp.dot(weights_low.T, grad_block, preferred_element_type=jnp.float32))
            weight_grad = jnp.dot(grad_block, value_seq[:block_end].T, preferred_element_type=jnp.float32)
            score_grad = (weights * (weight_grad - out_dot[block_start:block_end, None])).astype(jnp.bfloat16)
            query_pieces.append(jnp.dot(score_grad, key_seq[:block_end], preferred_element_type=jnp.float32) * score_scale)
            key_grad = key_grad.at[:block_end].add(jnp.dot(score_grad.T, query_seq[block_start:block_end], preferred_element_type=jnp.float32) * score_scale)
        return (jnp.concatenate(query_pieces, axis=0), key_grad, value_grad)
    head_inputs = (heads_first(queries), heads_first(keys), heads_first(values), heads_first(out_grad), heads_first(outputs))
    query_all, key_all, value_all = lax.map(one_head, head_inputs)

    def stored_order(per_head):
        return per_head.transpose(1, 0, 2).reshape(TOKENS, HEADS * HD)[positions].astype(jnp.bfloat16)
    return (stored_order(query_all), stored_order(key_all), stored_order(value_all))

def reference(queries, keys, values, out_grad, outputs, doc_ids, block_order):
    query_grad, key_grad, value_grad = lax.map(window_backward, (queries, keys, values, out_grad, outputs, doc_ids, block_order))
    return (query_grad, key_grad, value_grad)
```

```python
import functools
import math

import jax
import jax.numpy as jnp
from jax import lax
from jax.experimental import pallas as pl
from jax.experimental.pallas import tpu as pltpu
from jax.sharding import Mesh, PartitionSpec as P

HD = 128
BLOCK = 128
HEADS = 32
ROWS = 48
CHUNKS = 32
HALF = ROWS * CHUNKS
OWN_BLOCKS = HALF // BLOCK
ALL_BLOCKS = 2 * OWN_BLOCKS
PAD_BLOCKS = ALL_BLOCKS + 4
EXTRA = 16
SCALE = 1.0 / math.sqrt(HD)
SCALE_LOG2 = SCALE * math.log2(math.e)
NEG_FILL = -1e30
WINDOWS = ((2, 1), (4, 3), (8, 5), (12, 9))

CONTRACT_LAST = (((1,), (1,)), ((), ()))


def split_pair_kernel(first_ref, second_ref, out_ref):
    for head in range(HEADS):
        columns = slice(head * HD, (head + 1) * HD)
        out_ref[head, 0] = first_ref[:, columns]
        out_ref[head, 1] = second_ref[:, columns]


def split_pair(first, second):
    return pl.pallas_call(
        split_pair_kernel,
        out_shape=jax.ShapeDtypeStruct((HEADS, 2, ROWS, HD), jnp.bfloat16),
        name="split_pair",
    )(first, second)


def split_query_kernel(shift_ref, query_ref, grad_ref, output_ref, out_ref):
    lane = lax.broadcasted_iota(jnp.int32, (ROWS, HD), 1)
    dots = jnp.zeros((ROWS, HD), jnp.float32)
    for head in range(HEADS):
        columns = slice(head * HD, (head + 1) * HD)
        grad = grad_ref[:, columns]
        out_ref[head, 0:ROWS] = query_ref[:, columns]
        out_ref[head, ROWS : 2 * ROWS] = grad
        dot = jnp.sum(
            grad.astype(jnp.float32) * output_ref[:, columns].astype(jnp.float32),
            axis=1,
            keepdims=True,
        )
        dots = jnp.where(lane == head, dot, dots)
    by_head = jnp.concatenate([dots, jnp.zeros((HD - ROWS, HD), jnp.float32)], axis=0).T
    by_head = pltpu.roll(by_head[:HEADS], shift_ref[0], 1)
    high = by_head.astype(jnp.bfloat16).astype(jnp.float32)
    rest = by_head - high
    middle = rest.astype(jnp.bfloat16).astype(jnp.float32)
    low = rest - middle
    row = lax.broadcasted_iota(jnp.int32, (HEADS, EXTRA, HD), 1)
    parts = jnp.where(row == 0, high[:, None, :], 0.0)
    parts = jnp.where(row == 1, middle[:, None, :], parts)
    parts = jnp.where(row == 2, low[:, None, :], parts)
    out_ref[:, 2 * ROWS :, :] = parts.astype(jnp.bfloat16)


def split_query(shift, query, grad, output):
    return pl.pallas_call(
        split_query_kernel,
        out_shape=jax.ShapeDtypeStruct((HEADS, 2 * ROWS + EXTRA, HD), jnp.bfloat16),
        in_specs=[pl.BlockSpec(memory_space=pltpu.SMEM)]
        + [pl.BlockSpec(memory_space=pltpu.VMEM)] * 3,
        name="split_query",
    )(shift, query, grad, output)


def grads_kernel(
    meta_ref,
    queries_ref,
    own_ref,
    other_ref,
    query_grad_ref,
    own_grad_ref,
    other_grad_ref,
    query_s,
    grad_s,
    dot_s,
    key_s,
    value_s,
    keyt_s,
    key_acc,
    value_acc,
    dq_s,
):
    query_s[...] = queries_ref[:, 0:ROWS].reshape(HALF, HD)
    grad_s[...] = queries_ref[:, ROWS : 2 * ROWS].reshape(HALF, HD)
    parts = queries_ref[:, 2 * ROWS :].astype(jnp.float32)
    dots = parts[:, 0, :] + parts[:, 1, :] + parts[:, 2, :]
    lane = lax.broadcasted_iota(jnp.int32, (1, HD), 1)
    for group in range(4):
        piece = [dots[group * 8 + z : group * 8 + z + 1] for z in range(8)]
        blocks = (
            piece[0] + piece[1] + jnp.where(lane >= 96, piece[2], 0.0),
            jnp.where(lane < 16, piece[2], 0.0)
            + piece[3]
            + piece[4]
            + jnp.where(lane >= 112, piece[5], 0.0),
            jnp.where(lane < 32, piece[5], 0.0) + piece[6] + piece[7],
        )
        for index in range(3):
            dot_s[3 * group + index : 3 * group + index + 1, :] = blocks[index]
    tail = ALL_BLOCKS * BLOCK
    pad = (PAD_BLOCKS - ALL_BLOCKS) * BLOCK
    key_s[tail:, :] = jnp.zeros((pad, HD), jnp.bfloat16)
    value_s[tail:, :] = jnp.zeros((pad, HD), jnp.bfloat16)
    keyt_s[:, tail:] = jnp.zeros((HD, pad), jnp.bfloat16)
    key_acc[...] = jnp.zeros(key_acc.shape, jnp.float32)
    value_acc[...] = jnp.zeros(value_acc.shape, jnp.float32)
    for side, pair_ref in ((0, own_ref), (1, other_ref)):
        keys = pair_ref[:, 0].reshape(HALF, HD)
        values = pair_ref[:, 1].reshape(HALF, HD)
        for block in range(OWN_BLOCKS):
            rows = slice(block * BLOCK, (block + 1) * BLOCK)
            place = pl.multiple_of(meta_ref[0, side * OWN_BLOCKS + block] * BLOCK, BLOCK)
            key_s[pl.ds(place, BLOCK), :] = keys[rows]
            value_s[pl.ds(place, BLOCK), :] = values[rows]
            keyt_s[:, pl.ds(place, BLOCK)] = keys[rows].T

    def visit(block, width, fewest, position, first):
        rows = pl.ds(pl.multiple_of(block * BLOCK, BLOCK), BLOCK)
        span = pl.ds(pl.multiple_of(first * BLOCK, BLOCK), width * BLOCK)
        query = query_s[rows, :]
        grad = grad_s[rows, :]
        dot = dot_s[pl.ds(block, 1), :]
        scores = lax.dot_general(
            key_s[span, :], query, CONTRACT_LAST, preferred_element_type=jnp.float32
        )
        open_rows = (fewest - 1) * BLOCK
        shape = (width * BLOCK - open_rows, BLOCK)
        ahead = (
            lax.broadcasted_iota(jnp.int32, shape, 0)
            - lax.broadcasted_iota(jnp.int32, shape, 1)
            + open_rows
        )
        masked = jnp.where(ahead <= (position - first) * BLOCK, scores[open_rows:], NEG_FILL)
        if open_rows:
            scores = jnp.concatenate([scores[:open_rows], masked], axis=0)
        else:
            scores = masked
        highest = jnp.max(scores, axis=0, keepdims=True)
        weights = jnp.exp2((scores - highest) * SCALE_LOG2)
        weights = weights * (1.0 / jnp.sum(weights, axis=0, keepdims=True))
        value_acc[span, :] += jnp.dot(
            weights.astype(jnp.bfloat16), grad, preferred_element_type=jnp.float32
        )
        weight_grad = lax.dot_general(
            value_s[span, :], grad, CONTRACT_LAST, preferred_element_type=jnp.float32
        )
        score_grad = (weights * (weight_grad - dot)).astype(jnp.bfloat16)
        key_acc[span, :] += jnp.dot(score_grad, query, preferred_element_type=jnp.float32)
        turned = jnp.dot(keyt_s[:, span], score_grad, preferred_element_type=jnp.float32)
        dq_s[rows, :] = (turned.T * SCALE).astype(jnp.bfloat16)

    def step(block, carry):
        position = meta_ref[0, block]
        first = meta_ref[1, block]
        count = position - first + 1
        most = 0
        for width, fewest in WINDOWS:

            @pl.when((count > most) & (count <= width))
            def _(width=width, fewest=fewest):
                visit(block, width, fewest, position, first)

            most = width
        return carry

    lax.fori_loop(0, OWN_BLOCKS, step, 0)
    query_grad_ref[...] = dq_s[...].reshape(CHUNKS, ROWS, HD)
    for side, out_ref in ((0, own_grad_ref), (1, other_grad_ref)):
        for index, acc, factor in ((0, key_acc, SCALE), (1, value_acc, 1.0)):
            pieces = []
            for block in range(OWN_BLOCKS):
                place = pl.multiple_of(meta_ref[0, side * OWN_BLOCKS + block] * BLOCK, BLOCK)
                pieces.append((acc[pl.ds(place, BLOCK), :] * factor).astype(out_ref.dtype))
            out_ref[:, index] = jnp.concatenate(pieces, axis=0).reshape(CHUNKS, ROWS, HD)


def grads(meta, queries, own, other):
    pair_shape = (CHUNKS, 2, ROWS, HD)
    return pl.pallas_call(
        grads_kernel,
        out_shape=(
            jax.ShapeDtypeStruct((CHUNKS, ROWS, HD), jnp.bfloat16),
            jax.ShapeDtypeStruct(pair_shape, jnp.float32),
            jax.ShapeDtypeStruct(pair_shape, jnp.bfloat16),
        ),
        in_specs=[pl.BlockSpec(memory_space=pltpu.SMEM)]
        + [pl.BlockSpec(memory_space=pltpu.VMEM)] * 3,
        out_specs=[pl.BlockSpec(memory_space=pltpu.VMEM)] * 3,
        scratch_shapes=[
            pltpu.VMEM((HALF, HD), jnp.bfloat16),
            pltpu.VMEM((HALF, HD), jnp.bfloat16),
            pltpu.VMEM((16, HD), jnp.float32),
            pltpu.VMEM((PAD_BLOCKS * BLOCK, HD), jnp.bfloat16),
            pltpu.VMEM((PAD_BLOCKS * BLOCK, HD), jnp.bfloat16),
            pltpu.VMEM((HD, PAD_BLOCKS * BLOCK), jnp.bfloat16),
            pltpu.VMEM((PAD_BLOCKS * BLOCK, HD), jnp.float32),
            pltpu.VMEM((PAD_BLOCKS * BLOCK, HD), jnp.float32),
            pltpu.VMEM((HALF, HD), jnp.bfloat16),
        ],
        compiler_params=pltpu.CompilerParams(vmem_limit_bytes=40 * 1024 * 1024),
        name="grads",
    )(meta, queries, own, other)


def spread(value):
    return lax.all_to_all(value, ("x", "z"), 0, 0, tiled=True)


def swap(value):
    return lax.ppermute(value, "y", [(0, 1), (1, 0)])


def local(queries, keys, values, out_grad, outputs, doc_ids, block_order):
    side = lax.axis_index("y")
    order = block_order[0]
    documents = doc_ids[0]
    starts = jnp.sum((documents[None, :] < documents[:, None]).astype(jnp.int32), axis=1)
    own_first = jnp.where(
        side == 0, order, jnp.concatenate([order[OWN_BLOCKS:], order[:OWN_BLOCKS]])
    )
    table = lax.iota(jnp.int32, ALL_BLOCKS)
    first = jnp.sum(
        jnp.where(own_first[:, None] == table[None, :], starts[None, :], 0), axis=1
    )
    meta = jnp.stack([own_first, first])
    shift = jnp.reshape((lax.axis_index("z") * ROWS) % BLOCK, (1,)).astype(jnp.int32)

    own_pair = spread(split_pair(keys[0], values[0]))
    query_parts = spread(split_query(shift, queries[0], out_grad[0], outputs[0]))
    other_pair = swap(own_pair)
    query_grad, own_grad, other_grad = grads(meta, query_parts, own_pair, other_pair)
    arrived = swap(other_grad)
    query_back = spread(query_grad)
    pair_grad = (own_grad + arrived.astype(jnp.float32)).astype(jnp.bfloat16)
    pair_back = spread(pair_grad)

    def to_rows(by_head):
        return by_head.transpose(1, 0, 2).reshape(1, ROWS, HEADS * HD)

    return (to_rows(query_back), to_rows(pair_back[:, 0]), to_rows(pair_back[:, 1]))


def solution(mesh):
    grid = Mesh(mesh.devices.reshape(8, 4, 2, 4), ("z", "outer", "y", "x"))
    rows = P("outer", ("y", "x", "z"), None)
    whole = P("outer", None)
    return jax.shard_map(
        local,
        mesh=grid,
        in_specs=(rows, rows, rows, rows, rows, whole, whole),
        out_specs=(rows, rows, rows),
        check_vma=False,
    )
```

```python
import functools
import math

import jax
import jax.numpy as jnp
from jax import lax
from jax.experimental import pallas as pl
from jax.experimental.pallas import tpu as pltpu
from jax.sharding import Mesh, PartitionSpec as P

HD = 128
BLOCK = 128
HEADS = 32
ROWS = 48
CHUNKS = 32
HALF = ROWS * CHUNKS
OWN_BLOCKS = HALF // BLOCK
ALL_BLOCKS = 2 * OWN_BLOCKS
PAD_BLOCKS = ALL_BLOCKS + OWN_BLOCKS
EXTRA = 8
STAT_ROWS = 16
PAD_ROWS = (PAD_BLOCKS - ALL_BLOCKS) * BLOCK
SCALE = 1.0 / math.sqrt(HD)
SCALE_LOG2 = SCALE * math.log2(math.e)
NEG_FILL = -1e30
GROUP = 4
WINDOWS = (2, 4, 8, 12)

CORE0_GROUPS, CORE0_READY = (("k", "v"), ("q", "g")), True
CORE1_GROUPS, CORE1_READY = (("k", "v"), ("q", "g")), False

CONTRACT_LAST = (((1,), (1,)), ((), ()))


def dots_to_rows(shift_ref, dots, out_ref, first_row):
    by_head = jnp.concatenate([dots, jnp.zeros((HD - ROWS, HD), jnp.float32)], axis=0).T
    by_head = pltpu.roll(by_head[:HEADS], shift_ref[0], 1)
    high = by_head.astype(jnp.bfloat16).astype(jnp.float32)
    rest = by_head - high
    middle = rest.astype(jnp.bfloat16).astype(jnp.float32)
    low = rest - middle
    row = lax.broadcasted_iota(jnp.int32, (HEADS, EXTRA, HD), 1)
    parts = jnp.where(row == 0, high[:, None, :], 0.0)
    parts = jnp.where(row == 1, middle[:, None, :], parts)
    parts = jnp.where(row == 2, low[:, None, :], parts)
    out_ref[:, first_row:, :] = parts.astype(jnp.bfloat16)


def pack_kernel(with_dots, shift_ref, *refs):
    out_ref = refs[-1]
    copied = refs[:-2] if with_dots else refs[:-1]
    lane = lax.broadcasted_iota(jnp.int32, (ROWS, HD), 1)
    dots = jnp.zeros((ROWS, HD), jnp.float32)
    for head in range(HEADS):
        columns = slice(head * HD, (head + 1) * HD)
        for index, ref in enumerate(copied):
            out_ref[head, index * ROWS : (index + 1) * ROWS] = ref[:, columns]
        if with_dots:
            dot = jnp.sum(
                copied[-1][:, columns].astype(jnp.float32)
                * refs[-2][:, columns].astype(jnp.float32),
                axis=1,
                keepdims=True,
            )
            dots = jnp.where(lane == head, dot, dots)
    if with_dots:
        dots_to_rows(shift_ref, dots, out_ref, len(copied) * ROWS)


def pack(shift, arrays, outputs=None):
    with_dots = outputs is not None
    operands = [*arrays, outputs] if with_dots else [*arrays]
    rows = len(arrays) * ROWS + (EXTRA if with_dots else 0)
    return pl.pallas_call(
        functools.partial(pack_kernel, with_dots),
        out_shape=jax.ShapeDtypeStruct((HEADS, rows, HD), jnp.bfloat16),
        in_specs=[pl.BlockSpec(memory_space=pltpu.SMEM)]
        + [pl.BlockSpec(memory_space=pltpu.VMEM)] * len(operands),
        name="pack",
    )(shift, *operands)


def grads_kernel(groups, meta_ref, *refs):
    count = len(groups) + 1
    loaded_hbm, refs = refs[:count], refs[count:]
    (query_grad_hbm, own_grad_hbm, other_grad_hbm), refs = refs[:3], refs[3:]
    loaded, refs = refs[:count], refs[count:]
    query_grad_ref, own_grad_ref, other_grad_ref, *refs = refs
    query_s, grad_s, dot_s, key_s, value_s, keyt_s, key_acc, value_acc, dq_s, sem = refs
    loads = [
        pltpu.make_async_copy(source, target, sem.at[index])
        for index, (source, target) in enumerate(zip(loaded_hbm, loaded))
    ]
    for load in loads:
        load.start()
    rows_of = {}
    for ref, names in zip(loaded, (*groups, ("other_k", "other_v"))):
        for index, name in enumerate(names):
            rows_of[name] = ref, index * ROWS

    def rows(name):
        ref, first = rows_of[name]
        return ref[:, first : first + ROWS].reshape(HALF, HD)

    tail = ALL_BLOCKS * BLOCK
    key_s[tail:, :] = jnp.zeros((PAD_ROWS, HD), jnp.bfloat16)
    value_s[tail:, :] = jnp.zeros((PAD_ROWS, HD), jnp.bfloat16)
    keyt_s[:, tail:] = jnp.zeros((HD, PAD_ROWS), jnp.bfloat16)
    key_acc[...] = jnp.zeros(key_acc.shape, jnp.float32)
    value_acc[...] = jnp.zeros(value_acc.shape, jnp.float32)
    for load in loads:
        load.wait()
    for side, names in ((0, ("k", "v")), (1, ("other_k", "other_v"))):
        keys, values = rows(names[0]), rows(names[1])
        for block in range(OWN_BLOCKS):
            stored = slice(block * BLOCK, (block + 1) * BLOCK)
            place = pl.multiple_of(meta_ref[0, side * OWN_BLOCKS + block] * BLOCK, BLOCK)
            key_s[pl.ds(place, BLOCK), :] = keys[stored]
            value_s[pl.ds(place, BLOCK), :] = values[stored]
            keyt_s[:, pl.ds(place, BLOCK)] = keys[stored].T
    query_s[...] = rows("q")
    grad_s[...] = rows("g")
    last, first = rows_of["g"]
    parts = last[:, first + ROWS :].astype(jnp.float32)
    dots = parts[:, 0, :] + parts[:, 1, :] + parts[:, 2, :]
    lane = lax.broadcasted_iota(jnp.int32, (1, HD), 1)
    for group in range(4):
        piece = [dots[group * 8 + z : group * 8 + z + 1] for z in range(8)]
        blocks = (
            piece[0] + piece[1] + jnp.where(lane >= 96, piece[2], 0.0),
            jnp.where(lane < 16, piece[2], 0.0)
            + piece[3]
            + piece[4]
            + jnp.where(lane >= 112, piece[5], 0.0),
            jnp.where(lane < 32, piece[5], 0.0) + piece[6] + piece[7],
        )
        for index in range(3):
            dot_s[3 * group + index : 3 * group + index + 1, :] = blocks[index]

    def visit(blocks, width):
        shape = (width * BLOCK, BLOCK)
        ahead = lax.broadcasted_iota(jnp.int32, shape, 0) - lax.broadcasted_iota(
            jnp.int32, shape, 1
        )
        places, scores, weight_grads = [], [], []
        for block in blocks:
            first = meta_ref[1, block]
            rows = pl.ds(pl.multiple_of(block * BLOCK, BLOCK), BLOCK)
            span = pl.ds(pl.multiple_of(first * BLOCK, BLOCK), width * BLOCK)
            places.append((block, rows, span))
            score = lax.dot_general(
                key_s[span, :],
                query_s[rows, :],
                CONTRACT_LAST,
                preferred_element_type=jnp.float32,
            )
            reach = (meta_ref[0, block] - first) * BLOCK
            scores.append(jnp.where(ahead <= reach, score, NEG_FILL))
            weight_grads.append(
                lax.dot_general(
                    value_s[span, :],
                    grad_s[rows, :],
                    CONTRACT_LAST,
                    preferred_element_type=jnp.float32,
                )
                - dot_s[pl.ds(block, 1), :]
            )
        lows, score_grads = [], []
        for score, weight_grad in zip(scores, weight_grads):
            highest = jnp.max(score, axis=0, keepdims=True)
            weights = jnp.exp2((score - highest) * SCALE_LOG2)
            weights = weights * (1.0 / jnp.sum(weights, axis=0, keepdims=True))
            lows.append(weights.astype(jnp.bfloat16))
            score_grads.append((weights * weight_grad).astype(jnp.bfloat16))
        value_parts, key_parts = [], []
        for (_, rows, span), low, score_grad in zip(places, lows, score_grads):
            value_parts.append(jnp.dot(low, grad_s[rows, :], preferred_element_type=jnp.float32))
            key_parts.append(
                jnp.dot(score_grad, query_s[rows, :], preferred_element_type=jnp.float32)
            )
            turned = jnp.dot(keyt_s[:, span], score_grad, preferred_element_type=jnp.float32)
            dq_s[rows, :] = (turned.T * SCALE).astype(jnp.bfloat16)
        for (_, _, span), value_part, key_part in zip(places, value_parts, key_parts):
            value_acc[span, :] += value_part
            key_acc[span, :] += key_part

    def step(group, carry):
        blocks = [meta_ref[2, group * GROUP + member] for member in range(GROUP)]
        count = meta_ref[0, blocks[0]] - meta_ref[1, blocks[0]] + 1
        most = 0
        for width in WINDOWS:

            @pl.when((count > most) & (count <= width))
            def _(width=width):
                visit(blocks, width)

            most = width
        return carry

    lax.fori_loop(0, OWN_BLOCKS // GROUP, step, 0)
    stores = [
        pltpu.make_async_copy(source, target, sem.at[count + index])
        for index, (source, target) in enumerate(
            (
                (query_grad_ref, query_grad_hbm),
                (other_grad_ref, other_grad_hbm),
                (own_grad_ref, own_grad_hbm),
            )
        )
    ]
    query_grad_ref[...] = dq_s[...].reshape(CHUNKS, ROWS, HD)
    stores[0].start()
    for side, out_ref in ((1, other_grad_ref), (0, own_grad_ref)):
        for index, acc, factor in ((0, key_acc, SCALE), (1, value_acc, 1.0)):
            pieces = []
            for block in range(OWN_BLOCKS):
                place = pl.multiple_of(meta_ref[0, side * OWN_BLOCKS + block] * BLOCK, BLOCK)
                pieces.append((acc[pl.ds(place, BLOCK), :] * factor).astype(out_ref.dtype))
            out_ref[:, index * ROWS : (index + 1) * ROWS] = jnp.concatenate(
                pieces, axis=0
            ).reshape(CHUNKS, ROWS, HD)
        stores[2 - side].start()
    for store in stores:
        store.wait()


def grads(groups, meta, arrays, other):
    pair_shape = (CHUNKS, 2 * ROWS, HD)
    return pl.pallas_call(
        functools.partial(grads_kernel, groups),
        out_shape=(
            pltpu.HBM((CHUNKS, ROWS, HD), jnp.bfloat16),
            jax.ShapeDtypeStruct(pair_shape, jnp.float32),
            pltpu.HBM(pair_shape, jnp.bfloat16),
        ),
        in_specs=[pl.BlockSpec(memory_space=pltpu.SMEM)]
        + [pl.BlockSpec(memory_space=pl.ANY)] * (len(arrays) + 1),
        out_specs=[pl.BlockSpec(memory_space=pl.ANY)] * 3,
        scratch_shapes=[pltpu.VMEM(array.shape, jnp.bfloat16) for array in (*arrays, other)]
        + [
            pltpu.VMEM((CHUNKS, ROWS, HD), jnp.bfloat16),
            pltpu.VMEM(pair_shape, jnp.float32),
            pltpu.VMEM(pair_shape, jnp.bfloat16),
            pltpu.VMEM((HALF, HD), jnp.bfloat16),
            pltpu.VMEM((HALF, HD), jnp.bfloat16),
            pltpu.VMEM((STAT_ROWS, HD), jnp.float32),
            pltpu.VMEM((PAD_BLOCKS * BLOCK, HD), jnp.bfloat16),
            pltpu.VMEM((PAD_BLOCKS * BLOCK, HD), jnp.bfloat16),
            pltpu.VMEM((HD, PAD_BLOCKS * BLOCK), jnp.bfloat16),
            pltpu.VMEM((PAD_BLOCKS * BLOCK, HD), jnp.float32),
            pltpu.VMEM((PAD_BLOCKS * BLOCK, HD), jnp.float32),
            pltpu.VMEM((HALF, HD), jnp.bfloat16),
            pltpu.SemaphoreType.DMA((len(arrays) + 4,)),
        ],
        compiler_params=pltpu.CompilerParams(vmem_limit_bytes=24 * 1024 * 1024),
        name="grads",
    )(meta, *arrays, pltpu.with_memory_space_constraint(other, pltpu.HBM))


def spread(value):
    return lax.all_to_all(value, ("x", "z"), 0, 0, tiled=True)


def swap(value):
    return lax.ppermute(value, "y", [(0, 1), (1, 0)])


def tables(doc_ids, block_order):
    documents, order = doc_ids[0], block_order[0]
    starts = jnp.sum((documents[None, :] < documents[:, None]).astype(jnp.int32), axis=1)
    own_first = jnp.where(
        lax.axis_index("y") == 0,
        order,
        jnp.concatenate([order[OWN_BLOCKS:], order[:OWN_BLOCKS]]),
    )
    table = lax.iota(jnp.int32, ALL_BLOCKS)
    first = jnp.sum(
        jnp.where(own_first[:, None] == table[None, :], starts[None, :], 0), axis=1
    )
    length = (own_first - first)[:OWN_BLOCKS] * ALL_BLOCKS + table[:OWN_BLOCKS]
    rank = jnp.sum((length[None, :] > length[:, None]).astype(jnp.int32), axis=1)
    visits = jnp.sum(
        jnp.where(rank[None, :] == table[:, None], table[None, :OWN_BLOCKS], 0), axis=1
    )
    return jnp.stack([own_first, first, visits])


def to_rows(by_head):
    return by_head.transpose(1, 0, 2).reshape(1, ROWS, HEADS * HD)


def plan(groups, ready_first, queries, keys, values, out_grad, outputs, doc_ids, block_order):
    named = {"q": queries[0], "k": keys[0], "v": values[0], "g": out_grad[0]}
    shift = jnp.reshape((lax.axis_index("z") * ROWS) % BLOCK, (1,)).astype(jnp.int32)
    meta = tables(doc_ids, block_order)
    packed = [
        pack(shift, [named[name] for name in names], outputs[0] if "g" in names else None)
        for names in groups
    ]
    if ready_first:
        packed, meta = lax.optimization_barrier((packed, meta))
    arrays = [spread(group) for group in packed]
    other = swap(arrays[0][:, : 2 * ROWS])
    query_grad, own_grad, other_grad = grads(groups, meta, arrays, other)
    arrived = swap(other_grad)
    query_back = spread(query_grad)
    pair_grad = (own_grad + arrived.astype(jnp.float32)).astype(jnp.bfloat16)
    pair_back = spread(pair_grad)
    return (
        to_rows(query_back),
        to_rows(pair_back[:, :ROWS]),
        to_rows(pair_back[:, ROWS:]),
    )


def local(*arrays):
    return lax.cond(
        lax.axis_index("outer") % 2 == 0,
        functools.partial(plan, CORE0_GROUPS, CORE0_READY),
        functools.partial(plan, CORE1_GROUPS, CORE1_READY),
        *arrays,
    )


def solution(mesh):
    grid = Mesh(mesh.devices.reshape(8, 4, 2, 4), ("z", "outer", "y", "x"))
    rows = P("outer", ("y", "x", "z"), None)
    whole = P("outer", None)
    return jax.shard_map(
        local,
        mesh=grid,
        in_specs=(rows, rows, rows, rows, rows, whole, whole),
        out_specs=(rows, rows, rows),
        check_vma=False,
    )
```

```python
import functools
import math

import jax
import jax.numpy as jnp
from jax import lax
from jax.experimental import pallas as pl
from jax.experimental.pallas import tpu as pltpu
from jax.sharding import Mesh, PartitionSpec as P

HD = 128
BLOCK = 128
HEADS = 32
ROWS = 48
CHUNKS = 32
HALF = ROWS * CHUNKS
OWN_BLOCKS = HALF // BLOCK
ALL_BLOCKS = 2 * OWN_BLOCKS
PAD_BLOCKS = ALL_BLOCKS + OWN_BLOCKS
EXTRA = 8
STAT_ROWS = 16
PAD_ROWS = (PAD_BLOCKS - ALL_BLOCKS) * BLOCK
SCALE = 1.0 / math.sqrt(HD)
SCALE_LOG2 = SCALE * math.log2(math.e)
NEG_FILL = -1e30
GROUP = 4
WINDOWS = (2, 4, 6, 8, 12)
TOGETHER = (4, 8, 12)

GROUPS = (("k", "v"), ("q", "g"))

CONTRACT_LAST = (((1,), (1,)), ((), ()))


def dots_to_rows(shift_ref, dots, out_ref, first_row):
    by_head = jnp.concatenate([dots, jnp.zeros((HD - ROWS, HD), jnp.float32)], axis=0).T
    by_head = pltpu.roll(by_head[:HEADS], shift_ref[0], 1)
    high = by_head.astype(jnp.bfloat16).astype(jnp.float32)
    rest = by_head - high
    middle = rest.astype(jnp.bfloat16).astype(jnp.float32)
    low = rest - middle
    row = lax.broadcasted_iota(jnp.int32, (HEADS, EXTRA, HD), 1)
    parts = jnp.where(row == 0, high[:, None, :], 0.0)
    parts = jnp.where(row == 1, middle[:, None, :], parts)
    parts = jnp.where(row == 2, low[:, None, :], parts)
    out_ref[:, first_row:, :] = parts.astype(jnp.bfloat16)


def pack_kernel(with_dots, shift_ref, *refs):
    out_ref = refs[-1]
    copied = refs[:-2] if with_dots else refs[:-1]
    lane = lax.broadcasted_iota(jnp.int32, (ROWS, HD), 1)
    dots = jnp.zeros((ROWS, HD), jnp.float32)
    for head in range(HEADS):
        columns = slice(head * HD, (head + 1) * HD)
        for index, ref in enumerate(copied):
            out_ref[head, index * ROWS : (index + 1) * ROWS] = ref[:, columns]
        if with_dots:
            dot = jnp.sum(
                copied[-1][:, columns].astype(jnp.float32)
                * refs[-2][:, columns].astype(jnp.float32),
                axis=1,
                keepdims=True,
            )
            dots = jnp.where(lane == head, dot, dots)
    if with_dots:
        dots_to_rows(shift_ref, dots, out_ref, len(copied) * ROWS)


def pack(shift, arrays, outputs=None):
    with_dots = outputs is not None
    operands = [*arrays, outputs] if with_dots else [*arrays]
    rows = len(arrays) * ROWS + (EXTRA if with_dots else 0)
    return pl.pallas_call(
        functools.partial(pack_kernel, with_dots),
        out_shape=jax.ShapeDtypeStruct((HEADS, rows, HD), jnp.bfloat16),
        in_specs=[pl.BlockSpec(memory_space=pltpu.SMEM)]
        + [pl.BlockSpec(memory_space=pltpu.VMEM)] * len(operands),
        name="pack",
    )(shift, *operands)


def grads_kernel(groups, meta_ref, *refs):
    count = len(groups) + 1
    loaded_hbm, refs = refs[:count], refs[count:]
    (query_grad_hbm, own_grad_hbm, other_grad_hbm), refs = refs[:3], refs[3:]
    loaded, refs = refs[:count], refs[count:]
    query_grad_ref, own_grad_ref, other_grad_ref, *refs = refs
    query_s, grad_s, dot_s, key_s, value_s, keyt_s, key_acc, value_acc, dq_s, sem = refs
    loads = [
        pltpu.make_async_copy(source, target, sem.at[index])
        for index, (source, target) in enumerate(zip(loaded_hbm, loaded))
    ]
    for load in loads:
        load.start()
    rows_of = {}
    for ref, names in zip(loaded, (*groups, ("other_k", "other_v"))):
        for index, name in enumerate(names):
            rows_of[name] = ref, index * ROWS

    def rows(name):
        ref, first = rows_of[name]
        return ref[:, first : first + ROWS].reshape(HALF, HD)

    tail = ALL_BLOCKS * BLOCK
    key_s[tail:, :] = jnp.zeros((PAD_ROWS, HD), jnp.bfloat16)
    value_s[tail:, :] = jnp.zeros((PAD_ROWS, HD), jnp.bfloat16)
    keyt_s[:, tail:] = jnp.zeros((HD, PAD_ROWS), jnp.bfloat16)
    key_acc[...] = jnp.zeros(key_acc.shape, jnp.float32)
    value_acc[...] = jnp.zeros(value_acc.shape, jnp.float32)
    for load in loads[:-1]:
        load.wait()
    for side, names in ((0, ("k", "v")), (1, ("other_k", "other_v"))):
        if side == 1:
            loads[-1].wait()
        keys, values = rows(names[0]), rows(names[1])
        for block in range(OWN_BLOCKS):
            stored = slice(block * BLOCK, (block + 1) * BLOCK)
            place = pl.multiple_of(meta_ref[0, side * OWN_BLOCKS + block] * BLOCK, BLOCK)
            key_s[pl.ds(place, BLOCK), :] = keys[stored]
            value_s[pl.ds(place, BLOCK), :] = values[stored]
            keyt_s[:, pl.ds(place, BLOCK)] = keys[stored].T
    query_s[...] = rows("q")
    grad_s[...] = rows("g")
    last, first = rows_of["g"]
    parts = last[:, first + ROWS :].astype(jnp.float32)
    dots = parts[:, 0, :] + parts[:, 1, :] + parts[:, 2, :]
    lane = lax.broadcasted_iota(jnp.int32, (1, HD), 1)
    for group in range(4):
        piece = [dots[group * 8 + z : group * 8 + z + 1] for z in range(8)]
        blocks = (
            piece[0] + piece[1] + jnp.where(lane >= 96, piece[2], 0.0),
            jnp.where(lane < 16, piece[2], 0.0)
            + piece[3]
            + piece[4]
            + jnp.where(lane >= 112, piece[5], 0.0),
            jnp.where(lane < 32, piece[5], 0.0) + piece[6] + piece[7],
        )
        for index in range(3):
            dot_s[3 * group + index : 3 * group + index + 1, :] = blocks[index]

    def block_weights(block, ahead, scores, weight_grad):
        reach = (meta_ref[0, block] - meta_ref[1, block]) * BLOCK
        scores = jnp.where(ahead <= reach, scores, NEG_FILL)
        highest = jnp.max(scores, axis=0, keepdims=True)
        weights = jnp.exp2((scores - highest) * SCALE_LOG2)
        weights = weights * (1.0 / jnp.sum(weights, axis=0, keepdims=True))
        score_grad = weights * (weight_grad - dot_s[pl.ds(block, 1), :])
        return weights.astype(jnp.bfloat16), score_grad.astype(jnp.bfloat16)

    def visit(blocks, width, parts):
        shape = (width * BLOCK, BLOCK)
        ahead = lax.broadcasted_iota(jnp.int32, shape, 0) - lax.broadcasted_iota(
            jnp.int32, shape, 1
        )
        found = []
        for part in parts:
            members = [blocks[index] for index in part]
            places = [
                pl.ds(pl.multiple_of(block * BLOCK, BLOCK), BLOCK) for block in members
            ]
            first = pl.multiple_of(meta_ref[1, members[0]] * BLOCK, BLOCK)
            span = pl.ds(first, width * BLOCK)
            query = jnp.concatenate([query_s[rows, :] for rows in places], axis=0)
            grad = jnp.concatenate([grad_s[rows, :] for rows in places], axis=0)
            scores = lax.dot_general(
                key_s[span, :], query, CONTRACT_LAST, preferred_element_type=jnp.float32
            )
            weight_grads = lax.dot_general(
                value_s[span, :], grad, CONTRACT_LAST, preferred_element_type=jnp.float32
            )
            found.append((members, places, span, query, grad, scores, weight_grads))
        rounded = []
        for members, _, _, _, _, scores, weight_grads in found:
            pairs = [
                block_weights(
                    block,
                    ahead,
                    scores[:, index * BLOCK : (index + 1) * BLOCK],
                    weight_grads[:, index * BLOCK : (index + 1) * BLOCK],
                )
                for index, block in enumerate(members)
            ]
            rounded.append([jnp.concatenate(column, axis=1) for column in zip(*pairs)])
        sums = []
        for (_, places, span, query, grad, _, _), (low, score_grad) in zip(found, rounded):
            value_part = jnp.dot(low, grad, preferred_element_type=jnp.float32)
            key_part = jnp.dot(score_grad, query, preferred_element_type=jnp.float32)
            turned = jnp.dot(keyt_s[:, span], score_grad, preferred_element_type=jnp.float32)
            for index, rows in enumerate(places):
                columns = slice(index * BLOCK, (index + 1) * BLOCK)
                dq_s[rows, :] = (turned[:, columns].T * SCALE).astype(jnp.bfloat16)
            sums.append((span, value_part, key_part))
        for span, value_part, key_part in sums:
            value_acc[span, :] += value_part
            key_acc[span, :] += key_part

    def step(group, carry):
        blocks = [meta_ref[2, group * GROUP + member] for member in range(GROUP)]
        firsts = [meta_ref[1, block] for block in blocks]
        counts = [meta_ref[0, block] - first + 1 for block, first in zip(blocks, firsts)]
        count = functools.reduce(jnp.maximum, counts)
        alike = functools.reduce(
            jnp.logical_and, [first == firsts[0] for first in firsts[1:]]
        )
        apart = jnp.logical_not(alike)
        for chosen, widths, parts in (
            (alike, TOGETHER, (tuple(range(GROUP)),)),
            (apart, WINDOWS, tuple((member,) for member in range(GROUP))),
        ):
            most = 0
            for width in widths:

                @pl.when(chosen & (count > most) & (count <= width))
                def _(width=width, parts=parts):
                    visit(blocks, width, parts)

                most = width
        return carry

    lax.fori_loop(0, OWN_BLOCKS // GROUP, step, 0)
    stores = [
        pltpu.make_async_copy(source, target, sem.at[count + index])
        for index, (source, target) in enumerate(
            (
                (query_grad_ref, query_grad_hbm),
                (other_grad_ref, other_grad_hbm),
                (own_grad_ref, own_grad_hbm),
            )
        )
    ]
    query_grad_ref[...] = dq_s[...].reshape(CHUNKS, ROWS, HD)
    stores[0].start()
    for side, out_ref in ((1, other_grad_ref), (0, own_grad_ref)):
        for index, acc, factor in ((0, key_acc, SCALE), (1, value_acc, 1.0)):
            pieces = []
            for block in range(OWN_BLOCKS):
                place = pl.multiple_of(meta_ref[0, side * OWN_BLOCKS + block] * BLOCK, BLOCK)
                pieces.append((acc[pl.ds(place, BLOCK), :] * factor).astype(out_ref.dtype))
            out_ref[:, index * ROWS : (index + 1) * ROWS] = jnp.concatenate(
                pieces, axis=0
            ).reshape(CHUNKS, ROWS, HD)
        stores[2 - side].start()
    for store in stores:
        store.wait()


def grads(groups, meta, arrays, other):
    pair_shape = (CHUNKS, 2 * ROWS, HD)
    return pl.pallas_call(
        functools.partial(grads_kernel, groups),
        out_shape=(
            pltpu.HBM((CHUNKS, ROWS, HD), jnp.bfloat16),
            jax.ShapeDtypeStruct(pair_shape, jnp.float32),
            pltpu.HBM(pair_shape, jnp.bfloat16),
        ),
        in_specs=[pl.BlockSpec(memory_space=pltpu.SMEM)]
        + [pl.BlockSpec(memory_space=pl.ANY)] * (len(arrays) + 1),
        out_specs=[pl.BlockSpec(memory_space=pl.ANY)] * 3,
        scratch_shapes=[pltpu.VMEM(array.shape, jnp.bfloat16) for array in (*arrays, other)]
        + [
            pltpu.VMEM((CHUNKS, ROWS, HD), jnp.bfloat16),
            pltpu.VMEM(pair_shape, jnp.float32),
            pltpu.VMEM(pair_shape, jnp.bfloat16),
            pltpu.VMEM((HALF, HD), jnp.bfloat16),
            pltpu.VMEM((HALF, HD), jnp.bfloat16),
            pltpu.VMEM((STAT_ROWS, HD), jnp.float32),
            pltpu.VMEM((PAD_BLOCKS * BLOCK, HD), jnp.bfloat16),
            pltpu.VMEM((PAD_BLOCKS * BLOCK, HD), jnp.bfloat16),
            pltpu.VMEM((HD, PAD_BLOCKS * BLOCK), jnp.bfloat16),
            pltpu.VMEM((PAD_BLOCKS * BLOCK, HD), jnp.float32),
            pltpu.VMEM((PAD_BLOCKS * BLOCK, HD), jnp.float32),
            pltpu.VMEM((HALF, HD), jnp.bfloat16),
            pltpu.SemaphoreType.DMA((len(arrays) + 4,)),
        ],
        compiler_params=pltpu.CompilerParams(vmem_limit_bytes=24 * 1024 * 1024),
        name="grads",
    )(meta, *arrays, pltpu.with_memory_space_constraint(other, pltpu.HBM))


def spread(value):
    return lax.all_to_all(value, ("x", "z"), 0, 0, tiled=True)


def swap(value):
    return lax.ppermute(value, "y", [(0, 1), (1, 0)])


def tables(doc_ids, block_order):
    documents, order = doc_ids[0], block_order[0]
    starts = jnp.sum((documents[None, :] < documents[:, None]).astype(jnp.int32), axis=1)
    own_first = jnp.where(
        lax.axis_index("y") == 0,
        order,
        jnp.concatenate([order[OWN_BLOCKS:], order[:OWN_BLOCKS]]),
    )
    table = lax.iota(jnp.int32, ALL_BLOCKS)
    first = jnp.sum(
        jnp.where(own_first[:, None] == table[None, :], starts[None, :], 0), axis=1
    )
    sizes = jnp.sum((documents[None, :] == documents[:, None]).astype(jnp.int32), axis=1)
    size = jnp.sum(jnp.where(own_first[:, None] == table[None, :], sizes[None, :], 0), axis=1)
    length = (((size * ALL_BLOCKS) + own_first - first) * ALL_BLOCKS + table)[:OWN_BLOCKS]
    rank = jnp.sum((length[None, :] > length[:, None]).astype(jnp.int32), axis=1)
    visits = jnp.sum(
        jnp.where(rank[None, :] == table[:, None], table[None, :OWN_BLOCKS], 0), axis=1
    )
    return jnp.stack([own_first, first, visits])


def to_rows(by_head):
    return by_head.transpose(1, 0, 2).reshape(1, ROWS, HEADS * HD)


def first_leg(ready_first, queries, keys, values, out_grad, outputs, doc_ids, block_order):
    shift = jnp.reshape((lax.axis_index("z") * ROWS) % BLOCK, (1,)).astype(jnp.int32)
    meta = tables(doc_ids, block_order)
    pair = pack(shift, [keys[0], values[0]])
    query_parts = pack(shift, [queries[0], out_grad[0]], outputs[0])
    if ready_first:
        pair, query_parts, meta = lax.optimization_barrier((pair, query_parts, meta))
    return spread(pair), query_parts, meta


def local(*arrays):
    pair, query_parts, meta = lax.cond(
        lax.axis_index("outer") % 2 == 0,
        functools.partial(first_leg, True),
        functools.partial(first_leg, False),
        *arrays,
    )
    query_parts = spread(query_parts)
    other = swap(pair)
    query_grad, own_grad, other_grad = grads(GROUPS, meta, [pair, query_parts], other)
    arrived = swap(other_grad)
    query_back = spread(query_grad)
    pair_grad = (own_grad + arrived.astype(jnp.float32)).astype(jnp.bfloat16)
    pair_back = spread(pair_grad)
    return (
        to_rows(query_back),
        to_rows(pair_back[:, :ROWS]),
        to_rows(pair_back[:, ROWS:]),
    )


def solution(mesh):
    grid = Mesh(mesh.devices.reshape(8, 4, 2, 4), ("z", "outer", "y", "x"))
    rows = P("outer", ("y", "x", "z"), None)
    whole = P("outer", None)
    return jax.shard_map(
        local,
        mesh=grid,
        in_specs=(rows, rows, rows, rows, rows, whole, whole),
        out_specs=(rows, rows, rows),
        check_vma=False,
    )
```
